256 devices in a mesh: seq: 64 (over y, z_hi, x), sub: 4 (over z_lo, core).
Axes of the slice: x: 4, y: 4, z: 8 (z_hi: 4, z_lo: 2; z = z_hi * 2 + z_lo), core: 2. Of those that a mesh axis runs over, the one named last changes fastest.
Arguments:
- queries: bfloat16 [65536, 1024], P(('seq', 'sub')), may hold values from -8 to 8
- keys: bfloat16 [65536, 1024], P(('seq', 'sub')), may hold values from -8 to 8
- values: bfloat16 [65536, 1024], P(('seq', 'sub')), may hold values from -8 to 8
Outputs:
- attended: bfloat16 [65536, 1024], P(('seq', 'sub'))
The draws below stay inside these ranges and needn't reach their ends.
All inputs are finite; a program needn't handle non-finite values.
Results may differ from the reference program's by a relative error of at most 0.0018.
Values may be sent and summed in bfloat16 or wider, within the bound.
A program may use at most 64 MiB of HBM per device.

```python
import math
import jax
import jax.numpy as jnp
from jax import lax

HEADS = 8
HEAD = 128
LEAF = 128
TOK_DEV = 256
TOKENS = 65536
SHIFT = 1
DEPTH = 8


def multiscale(key):
    feat_width = HEADS * HEAD
    scale_count = TOKENS.bit_length()
    summed = jnp.zeros((TOKENS, feat_width), jnp.float32)
    for s in range(scale_count):
        layer_key = jax.random.fold_in(key, 100 + s)
        row_count = TOKENS >> s
        gauss = jax.random.normal(jax.random.fold_in(layer_key, 1), (row_count, feat_width), jnp.float32)
        layer_piece = gauss
        summed = summed + jnp.repeat(layer_piece, 1 << s, axis=0)
    return summed / math.sqrt(scale_count)


def draw_queries(key, part):
    key = jax.random.fold_in(key, 1)
    feat_width = HEADS * HEAD
    drawn = jax.random.normal(key, (TOKENS, feat_width), jnp.float32)
    return jnp.clip(drawn, -8.0, 8.0).astype(jnp.bfloat16)


def draw_keys(key, part):
    key = jax.random.fold_in(key, 2)
    drawn = multiscale(key)
    return jnp.clip(drawn, -8.0, 8.0).astype(jnp.bfloat16)


def draw_values(key, part):
    key = jax.random.fold_in(key, 3)
    drawn = multiscale(key)
    return jnp.clip(drawn, -8.0, 8.0).astype(jnp.bfloat16)


def setup_inputs(seed: int = 0) -> dict:
    arg_keys = jax.random.split(jax.random.key(seed), 4)
    return {
        "queries": draw_queries(jax.random.fold_in(arg_keys[3], 71), 0),
        "keys": draw_keys(jax.random.fold_in(arg_keys[3], 71), 0),
        "values": draw_values(jax.random.fold_in(arg_keys[3], 71), 0),
    }


def attend(queries_blk, keys_blk, values_blk, visible):
    score_scale = 1.0 / math.sqrt(queries_blk.shape[-1])
    scores = jnp.einsum('gqhe,gkhe->gqhk', queries_blk.astype(jnp.float32), keys_blk.astype(jnp.float32)) * score_scale
    if visible is not None:
        scores = jnp.where(visible[:, None, None, :], scores, -jnp.inf)
    highest = lax.optimization_barrier(jnp.max(scores, axis=-1))
    exp_scores = jnp.exp(scores - highest[..., None])
    denominator = lax.optimization_barrier(jnp.sum(exp_scores, axis=-1))
    weights = exp_scores.astype(jnp.bfloat16)
    numerator = jnp.einsum('gqhk,gkhe->gqhe', weights.astype(jnp.float32), values_blk.astype(jnp.float32))
    return (highest, denominator, numerator)

def flatten(result, tok_rows):
    highest, denominator, numerator = result
    return (highest.reshape(tok_rows, -1), denominator.reshape(tok_rows, -1), numerator.reshape(tok_rows, numerator.shape[-2], numerator.shape[-1]))

def combine(running, fresh):
    old_max, old_total, old_sum = running
    new_max, new_total, new_sum = fresh
    joint_max = jnp.maximum(old_max, new_max)
    old_factor = jnp.exp(old_max - joint_max)
    new_factor = jnp.exp(new_max - joint_max)
    return (joint_max, old_factor * old_total + new_factor * new_total, old_factor[..., None] * old_sum + new_factor[..., None] * new_sum)

def reference(queries, keys, values):
    feat_width = HEADS * HEAD
    level_count = SHIFT + DEPTH - 1
    stacked = jnp.stack((keys, values))
    coarse_levels = []
    current = 0.5 * lax.optimization_barrier(jnp.sum(stacked.reshape(2, TOKENS // 2, 2, feat_width).astype(jnp.float32), axis=2))
    for l in range(1, level_count + 1):
        if l > 1:
            current = 0.5 * lax.optimization_barrier(jnp.sum(current.reshape(2, -1, 2, feat_width), axis=2))
        coarse_levels.append(current.astype(jnp.bfloat16))
    padded = jnp.pad(stacked, ((0, 0), (LEAF, LEAF), (0, 0)))
    leaf_blocks = TOK_DEV // LEAF

    def one_slab(slab_index):
        first_row = (slab_index * TOK_DEV).astype(jnp.int32)
        slab_queries = lax.dynamic_slice_in_dim(queries, first_row, TOK_DEV, 0)
        near = lax.dynamic_slice_in_dim(padded, first_row, TOK_DEV + 2 * LEAF, 1)
        windows = jnp.concatenate([near[:, o:o + TOK_DEV].reshape(2, leaf_blocks, LEAF, HEADS, HEAD) for o in (0, LEAF, 2 * LEAF)], axis=2)
        offsets = jnp.arange(leaf_blocks, dtype=jnp.int32)[:, None] * LEAF + jnp.arange(3 * LEAF, dtype=jnp.int32)[None, :] - LEAF + first_row
        visible = (offsets >= 0) & (offsets < TOKENS)
        running = flatten(attend(slab_queries.reshape(leaf_blocks, LEAF, HEADS, HEAD), windows[0], windows[1], visible), TOK_DEV)
        for l in range(1, level_count + 1):
            coarse = coarse_levels[l - 1]
            if l < SHIFT:
                coarse_rows = TOK_DEV // 2 ** l
                groups = coarse_rows // LEAF
                own_rows = lax.dynamic_slice_in_dim(coarse, (first_row // 2 ** l).astype(jnp.int32), coarse_rows, 1)
                sibling = own_rows.reshape(2, groups // 2, 2, LEAF, HEADS, HEAD)[:, :, ::-1].reshape(2, groups, LEAF, HEADS, HEAD)
                query_groups = slab_queries.reshape(groups, LEAF * 2 ** l, HEADS, HEAD)
            else:
                partner = jnp.bitwise_xor(jnp.right_shift(slab_index, l - SHIFT), 1)
                sibling = lax.dynamic_slice_in_dim(coarse, (partner * LEAF).astype(jnp.int32), LEAF, 1).reshape(2, 1, LEAF, HEADS, HEAD)
                query_groups = slab_queries.reshape(1, TOK_DEV, HEADS, HEAD)
            running = combine(running, flatten(attend(query_groups, sibling[0], sibling[1], None), TOK_DEV))
        highest, denominator, numerator = running
        return (numerator / denominator[..., None]).reshape(TOK_DEV, feat_width).astype(jnp.bfloat16)
    slabs = lax.map(one_slab, jnp.arange(TOKENS // TOK_DEV, dtype=jnp.int32))
    return slabs.reshape(TOKENS, feat_width)
```

```python
import math

import jax
import jax.numpy as jnp
from jax import lax
from jax.experimental import pallas as pl
from jax.experimental.pallas import tpu as pltpu
from jax.sharding import PartitionSpec as P

HEADS = 8
HEAD = 128
LEAF = 128
TOK = 256
FEAT = HEADS * HEAD
UNIT = 2 * HEADS
X, Y, Z, CORES = 4, 4, 8, 2
MESH = pl.DeviceIdType.MESH
F32 = jnp.float32
BF16 = jnp.bfloat16
EXP2_SCALE = math.log2(math.e) / math.sqrt(HEAD)
HIDDEN = -1e30


def averaging_matrix():
    row = lax.broadcasted_iota(jnp.int32, (TOK, TOK), 0)
    tok = lax.broadcasted_iota(jnp.int32, (TOK, TOK), 1)
    result = jnp.zeros((TOK, TOK), F32)
    base = 0
    for level in range(1, 9):
        count = TOK >> level
        first = (row - base) * (1 << level)
        hit = (row >= base) & (row < base + count) & (tok >= first) & (tok < first + (1 << level))
        result = jnp.where(hit, 2.0**-level, result)
        base += count
    return result.astype(BF16)


def kernel(
    q_hbm,
    k_hbm,
    v_hbm,
    out_ref,
    q,
    kv,
    halo,
    own,
    lvl,
    unit,
    zbuf,
    t5,
    t6,
    t7,
    t8,
    spread,
    wide,
    acc,
    top,
    total,
    in_sem,
    send_sem,
    recv_sem,
):
    seq, sub = lax.axis_index("seq"), lax.axis_index("sub")
    x = lax.rem(seq, X)
    zhi = lax.rem(seq // X, Z // 2)
    y = seq // (X * Z // 2)
    c = lax.rem(sub, CORES)
    zlo = sub // CORES
    z = zhi * 2 + zlo
    place = seq * 4 + sub

    def at(xx, yy, zz, cc):
        return {"seq": (yy * (Z // 2) + zz // 2) * X + xx, "sub": lax.rem(zz, 2) * CORES + cc}

    def linear(pos):
        return {"seq": pos // 4, "sub": lax.rem(pos, 4)}

    loads = [
        pltpu.make_async_copy(k_hbm, kv.at[0], in_sem.at[0]),
        pltpu.make_async_copy(v_hbm, kv.at[1], in_sem.at[1]),
        pltpu.make_async_copy(q_hbm, q, in_sem.at[2]),
    ]
    for load in loads:
        load.start()

    x1 = x + 1 - 2 * lax.rem(x, 2)
    y1 = y + 1 - 2 * lax.rem(y, 2)
    z1 = z + 1 - 2 * zlo
    mate = at(x, y, z, 1 - c)
    x_peers = [lax.rem(x + d, X) for d in (1, 2, 3)]
    x_far = [(1 - x // 2) * 2 + j for j in range(2)]
    y_far = [(1 - y // 2) * 2 + j for j in range(2)]
    z_peers = [lax.rem(z + d, Z) for d in range(1, Z)]
    zhi1 = zhi + 1 - 2 * lax.rem(zhi, 2)
    z_near = [zhi1 * 2 + j for j in range(2)]
    z_far = [(1 - zhi // 2) * 4 + j for j in range(4)]
    before = linear(lax.rem(place + 255, 256))
    after = linear(lax.rem(place + 1, 256))
    ends = linear(lax.rem(place + 1 + 254 * (1 - c), 256))

    barrier = pltpu.get_barrier_semaphore()
    greeted = [mate, ends]
    greeted += [at(xx, y, z, c) for xx in x_peers] + [at(xx, y, z1, c) for xx in x_peers]
    greeted += [at(x, yy, z, c) for yy in [y1] + y_far]
    greeted += [at(x, y, zz, c) for zz in z_peers]
    for peer in greeted:
        pl.semaphore_signal(barrier, inc=1, device_id=peer, device_id_type=MESH)

    loads[0].wait()
    loads[1].wait()
    average = averaging_matrix()
    for i in range(2):
        for j in range(4):
            cols = pl.ds(j * 256, 256)
            coarse = jnp.dot(average, kv[i, :, cols], preferred_element_type=F32)
            own[i, :, cols] = coarse.astype(BF16)
            for hh in range(2):
                spread[pl.ds((i * HEADS + j * 2 + hh) * 16, 16), :] = coarse[240:, hh * HEAD : (hh + 1) * HEAD]
    for r in range(16):
        unit[r] = spread[pl.ds(r, UNIT, stride=16), :].astype(BF16)
    zbuf[z] = unit[12:15]

    pl.semaphore_wait(barrier, len(greeted))

    started = []

    def send(src, dst, recv, peer):
        copy = pltpu.make_async_remote_copy(
            src_ref=src,
            dst_ref=dst,
            send_sem=send_sem.at[len(started)],
            recv_sem=recv_sem.at[recv],
            device_id=peer,
            device_id_type=MESH,
        )
        copy.start()
        started.append(copy)

    def arrived(ref, recv):
        pltpu.make_async_copy(ref, ref, recv_sem.at[recv]).wait()

    mine = pl.ds(pl.multiple_of(c * 64, 64), 64)
    for zz in z_peers:
        send(unit.at[pl.ds(12, 3)], zbuf.at[z], 0, at(x, y, zz, c))
    for zz in z_far:
        send(unit.at[pl.ds(8, 4)], t6.at[c, x, lax.rem(z, 4)], 1, at(x, y, zz, c))
    for zz in z_near:
        send(unit.at[pl.ds(0, 8)], t5.at[c, x, zlo], 2, at(x, y, zz, c))
    slot = pl.ds(pl.multiple_of(c * 64 + (lax.rem(x, 2) * 2 + zlo) * 16, 16), 16)
    for xx in x_far:
        for zz in (z, z1):
            send(own.at[:, pl.ds(224, 16)], lvl.at[3, :, slot], 3, at(xx, y, zz, c))
    slot = pl.ds(pl.multiple_of(c * 64 + zlo * 32, 32), 32)
    for zz in (z, z1):
        send(own.at[:, pl.ds(192, 32)], lvl.at[2, :, slot], 4, at(x1, y, zz, c))
    send(own.at[:, pl.ds(128, 64)], lvl.at[1, :, mine], 5, at(x, y, z1, c))
    send(own.at[:, pl.ds(0, 128)], lvl.at[0], 6, mate)
    send(kv.at[:, pl.ds(LEAF, LEAF)], halo.at[0], 7, after)
    send(kv.at[:, pl.ds(0, LEAF)], halo.at[1], 8, before)

    def update(h, scores, values, first=False):
        high = jnp.max(scores, axis=0, keepdims=True)
        if first:
            joint = high
        else:
            old = top[h]
            joint = jnp.maximum(old, high)
            factor = jnp.exp2((old - joint) * EXP2_SCALE)
        weights = jnp.exp2((scores - joint) * EXP2_SCALE)
        weight_sum = jnp.sum(weights, axis=0, keepdims=True)
        fresh = weights.astype(BF16)
        fresh = values(fresh)
        if first:
            total[h] = weight_sum
            acc[h] = fresh
        else:
            total[h] = total[h] * factor + weight_sum
            acc[h] = acc[h] * factor + fresh
        top[h] = joint

    def scored(keys, queries):
        return lax.dot_general(keys, queries, (((1,), (1,)), ((), ())), preferred_element_type=F32)

    def weighted(values, weights):
        return lax.dot_general(values, weights, (((0,), (0,)), ((), ())), preferred_element_type=F32)

    def for_heads(body):
        for h in range(HEADS):
            body(h, pl.ds(h * HEAD, HEAD))

    arrived(zbuf.at[pl.ds(0, 7)], 0)
    send(zbuf.at[:, pl.ds(0, 2)], t7.at[c, x], 9, at(x, y1, z, c))
    for yy in y_far:
        send(zbuf.at[:, 2], t8.at[c, x, lax.rem(y, 2)], 10, at(x, yy, z, c))
    arrived(t6.at[c, x], 1)
    for d in range(3):
        send(t6.at[c, x], t6.at[c, x], 11, at(x_peers[d], y, z, c))
    arrived(t5.at[c, x], 2)
    for d in range(3):
        send(t5.at[c, x], t5.at[c, x], 12, at(x_peers[d], y, z, c))

    loads[2].wait()

    def own_tokens(h, cols):
        scores = scored(kv[0, :, cols], q[:, cols])
        update(h, scores, lambda w: weighted(kv[1, :, cols], w), first=True)

    for_heads(own_tokens)

    arrived(t7.at[c, x], 9)
    for d in range(3):
        send(t7.at[c, x], t7.at[c, x], 13, at(x_peers[d], y, z, c))
    arrived(t8.at[c, x], 10)
    for d in range(3):
        send(t8.at[c, x], t8.at[c, x], 14, at(x_peers[d], y, z, c))

    def level(number):
        def body(h, cols):
            scores = scored(lvl[number, 0, :, cols], q[:, cols])
            update(h, scores, lambda w: weighted(lvl[number, 1, :, cols], w))

        for_heads(body)

    arrived(lvl.at[0], 6)
    level(0)

    for number, recv in ((3, 3), (2, 4), (1, 5)):
        arrived(lvl.at[number, :, mine], recv)
        send(lvl.at[number, :, mine], lvl.at[number, :, mine], 15 + number, mate)

    other = pl.ds(pl.multiple_of((1 - c) * 64, 64), 64)
    for number in (3, 2, 1):
        arrived(lvl.at[number, :, other], 15 + number)
        level(number)

    deep = ((t6, 11, 19), (t5, 12, 20), (t7, 13, 21), (t8, 14, 22))
    for tiles, recv, handed in deep:
        arrived(tiles.at[c, pl.ds(0, 3)], recv)
        send(tiles.at[c], tiles.at[c], handed, mate)

    arrived(halo.at[0], 7)
    arrived(halo.at[1], 8)
    has_before = place > 0
    has_after = place < 255
    lane = lax.broadcasted_iota(jnp.int32, (1, TOK), 1)
    seen = ((lane < LEAF) & has_before) | ((lane >= LEAF) & has_after)

    def halos(h, cols):
        scores = jnp.concatenate(
            [scored(halo[0, 0, :, cols], q[:LEAF, cols]), scored(halo[1, 0, :, cols], q[LEAF:, cols])], axis=1
        )
        scores = jnp.where(seen, scores, HIDDEN)
        update(
            h,
            scores,
            lambda w: jnp.concatenate(
                [weighted(halo[0, 1, :, cols], w[:, :LEAF]), weighted(halo[1, 1, :, cols], w[:, LEAF:])], axis=1
            ),
        )

    for_heads(halos)

    for tiles, _, handed in deep:
        arrived(tiles.at[1 - c], handed)
        wide[...] = tiles[...].astype(F32).reshape(LEAF * UNIT, HEAD)

        def body(h, cols):
            keys = wide[pl.ds(h, LEAF, stride=UNIT), :].astype(BF16)
            scores = scored(keys, q[:, cols])
            update(
                h, scores, lambda w: weighted(wide[pl.ds(HEADS + h, LEAF, stride=UNIT), :].astype(BF16), w)
            )

        for_heads(body)

    def finish(h, cols):
        out_ref[:, cols] = (acc[h] / total[h]).T.astype(BF16)

    for_heads(finish)

    for copy in started:
        copy.wait_send()


def on_device(queries, keys, values):
    return pl.pallas_call(
        kernel,
        out_shape=jax.ShapeDtypeStruct((TOK, FEAT), BF16),
        in_specs=[pl.BlockSpec(memory_space=pl.ANY)] * 3,
        out_specs=pl.BlockSpec(memory_space=pltpu.VMEM),
        scratch_shapes=[
            pltpu.VMEM((TOK, FEAT), BF16),
            pltpu.VMEM((2, TOK, FEAT), BF16),
            pltpu.VMEM((2, 2, LEAF, FEAT), BF16),
            pltpu.VMEM((2, TOK, FEAT), BF16),
            pltpu.VMEM((4, 2, LEAF, FEAT), BF16),
            pltpu.VMEM((16, UNIT, HEAD), BF16),
            pltpu.VMEM((Z, 3, UNIT, HEAD), BF16),
            pltpu.VMEM((CORES, X, 2, 8, UNIT, HEAD), BF16),
            pltpu.VMEM((CORES, X, 4, 4, UNIT, HEAD), BF16),
            pltpu.VMEM((CORES, X, Z, 2, UNIT, HEAD), BF16),
            pltpu.VMEM((CORES, X, 2, Z, UNIT, HEAD), BF16),
            pltpu.VMEM((TOK, HEAD), F32),
            pltpu.VMEM((LEAF * UNIT, HEAD), F32),
            pltpu.VMEM((HEADS, HEAD, TOK), F32),
            pltpu.VMEM((HEADS, 1, TOK), F32),
            pltpu.VMEM((HEADS, 1, TOK), F32),
            pltpu.SemaphoreType.DMA((3,)),
            pltpu.SemaphoreType.DMA((64,)),
            pltpu.SemaphoreType.DMA((23,)),
        ],
        compiler_params=pltpu.CompilerParams(
            collective_id=0, has_side_effects=True, vmem_limit_bytes=48 * 1024 * 1024
        ),
    )(queries, keys, values)


def solution(mesh):
    spec = P(("seq", "sub"), None)
    return jax.shard_map(on_device, mesh=mesh, in_specs=(spec, spec, spec), out_specs=spec, check_vma=False)
```

```python
import math

import jax
import jax.numpy as jnp
from jax import lax
from jax.experimental import pallas as pl
from jax.experimental.pallas import tpu as pltpu
from jax.sharding import PartitionSpec as P

HEADS = 8
HEAD = 128
LEAF = 128
TOK = 256
FEAT = HEADS * HEAD
UNIT = 2 * HEADS
X, Y, Z, CORES = 4, 4, 8, 2
MESH = pl.DeviceIdType.MESH
F32 = jnp.float32
BF16 = jnp.bfloat16
EXP2_SCALE = math.log2(math.e) / math.sqrt(HEAD)
HIDDEN = -1e30


def averaging_matrix():
    row = lax.broadcasted_iota(jnp.int32, (TOK, TOK), 0)
    tok = lax.broadcasted_iota(jnp.int32, (TOK, TOK), 1)
    result = jnp.zeros((TOK, TOK), F32)
    base = 0
    for level in range(1, 9):
        count = TOK >> level
        first = (row - base) * (1 << level)
        hit = (row >= base) & (row < base + count) & (tok >= first) & (tok < first + (1 << level))
        result = jnp.where(hit, 2.0**-level, result)
        base += count
    return result.astype(BF16)


def kernel(
    q_hbm,
    k_hbm,
    v_hbm,
    out_ref,
    q,
    kv,
    halo,
    transit,
    own,
    lvl,
    derived,
    unit,
    ybuf,
    zbuf,
    t5,
    t6,
    t7,
    t8,
    spread,
    wide,
    acc,
    top,
    total,
    in_sem,
    send_sem,
    recv_sem,
    near_sem,
    far_sem,
):
    seq, sub = lax.axis_index("seq"), lax.axis_index("sub")
    x = lax.rem(seq, X)
    zhi = lax.rem(seq // X, Z // 2)
    y = seq // (X * Z // 2)
    c = lax.rem(sub, CORES)
    zlo = sub // CORES
    z = zhi * 2 + zlo
    place = seq * 4 + sub

    def at(xx, yy, zz, cc):
        return {"seq": (yy * (Z // 2) + zz // 2) * X + xx, "sub": lax.rem(zz, 2) * CORES + cc}

    loads = [
        pltpu.make_async_copy(k_hbm, kv.at[0], in_sem.at[0]),
        pltpu.make_async_copy(v_hbm, kv.at[1], in_sem.at[1]),
        pltpu.make_async_copy(q_hbm, q, in_sem.at[2]),
    ]
    for load in loads:
        load.start()

    x1 = x + 1 - 2 * lax.rem(x, 2)
    x3 = X - 1 - x
    y1 = y + 1 - 2 * lax.rem(y, 2)
    y2 = lax.rem(y + 2, Y)
    yp = lax.rem(y, 2)
    z1 = z + 1 - 2 * zlo
    mate = at(x, y, z, 1 - c)
    zhi1 = zhi + 1 - 2 * lax.rem(zhi, 2)
    end_place = lax.rem(place + 1 + 254 * (1 - c), 256)
    end = {"seq": end_place // 4, "sub": lax.rem(end_place, 4)}
    end_zhi = lax.rem(end_place // 16, Z // 2)
    end_near = end_zhi == zhi

    cross = at(x, y, z1, 1 - c)
    near = [(mate, c == 0), (at(x, y, z1, c), zlo == 0), (cross, zlo == 0), (at(x, y1, z, c), y1 > y), (at(x, y2, z, c), y2 > y)]
    near += [(at(xx, y, z, c), xx > x) for xx in [lax.rem(x + d, X) for d in (1, 2, 3)]]
    far_peers = [
        (at(x, y, zz * 2 + j, c), zz > zhi) for zz in [lax.rem(zhi + d, Z // 2) for d in (3, 2, 1)] for j in range(2)
    ]
    others = [peer for peer, _ in far_peers]
    end_far = jnp.logical_not(end_near)
    far_peers += [(end, end_zhi > zhi)]

    barrier = pltpu.get_barrier_semaphore()

    def tell(sem, peer, when):
        @pl.when(when)
        def _():
            pl.semaphore_signal(sem, inc=1, device_id=peer, device_id_type=MESH)

    def count(flags):
        return sum(flag.astype(jnp.int32) for flag in flags)

    def await_count(sem, amount):
        @pl.when(amount > 0)
        def _():
            pl.semaphore_wait(sem, amount)

    for peer, later in far_peers + near:
        tell(barrier, peer, later)
    await_count(
        barrier,
        count([jnp.logical_not(later) for _, later in near + far_peers[:-1]]) + (end_zhi < zhi).astype(jnp.int32),
    )
    for peer, later in far_peers[:-1]:
        tell(far_sem, peer, jnp.logical_not(later))
    tell(far_sem, end, end_zhi < zhi)
    for peer, later in near:
        tell(near_sem, peer, jnp.logical_not(later))

    loads[0].wait()
    loads[1].wait()
    average = averaging_matrix()
    for i in range(2):
        for j in range(4):
            cols = pl.ds(j * 256, 256)
            coarse = jnp.dot(average, kv[i, :, cols], preferred_element_type=F32)
            own[i, :, cols] = coarse.astype(BF16)
            for hh in range(2):
                spread[pl.ds((i * HEADS + j * 2 + hh) * 16, 16), :] = coarse[240:, hh * HEAD : (hh + 1) * HEAD]
    for r in range(16):
        unit[r] = spread[pl.ds(r, UNIT, stride=16), :].astype(BF16)

    await_count(near_sem, count([later for _, later in near]))

    started = []

    def copy_to(src, dst, recv, peer, slot):
        return pltpu.make_async_remote_copy(
            src_ref=src,
            dst_ref=dst,
            send_sem=send_sem.at[slot],
            recv_sem=recv_sem.at[recv],
            device_id=peer,
            device_id_type=MESH,
        )

    def send(src, dst, recv, peer):
        copy = copy_to(src, dst, recv, peer, 14 + len(started))
        copy.start()
        started.append(copy)

    def arrived(ref, recv):
        pltpu.make_async_copy(ref, ref, recv_sem.at[recv]).wait()

    def rows(start, count):
        return pl.ds(pl.multiple_of(start, 16), count)

    mine, other = rows(c * 64, 64), rows((1 - c) * 64, 64)
    outer = c == zlo
    edge = kv.at[:, rows(c * LEAF, LEAF)]
    end_copy = copy_to(edge, halo.at[1 - c], 7, end, 0)
    inner_copy = copy_to(edge, halo.at[1 - c], 7, cross, 0)
    step_copy = copy_to(edge, transit, 43, at(lax.rem(x + 3 + 2 * c, X), y, z, c), 0)
    pass_copy = copy_to(transit, halo.at[1 - c], 7, cross, 100)
    steps = outer & end_near
    passes = outer & (x != 3 * (1 - c))
    far = [copy_to(unit.at[pl.ds(8, 4)], t6.at[c, x, lax.rem(z, 4)], 9, at(x, y, (1 - zhi // 2) * 4 + j, c), 1 + j) for j in range(4)]
    far += [copy_to(unit.at[pl.ds(0, 8)], t5.at[c, x, zlo], 8, at(x, y, zhi1 * 2 + j, c), 5 + j) for j in range(2)]
    gather = [copy_to(ybuf, zbuf.at[z], 10, peer, 7 + j) for j, peer in enumerate(others + [at(x, y, z1, c)])]

    def update(h, lanes, scores, values, first=False):
        high = jnp.max(scores, axis=0, keepdims=True)
        if first:
            joint = high
        else:
            old = top[h, :, lanes]
            joint = jnp.maximum(old, high)
            factor = jnp.exp2((old - joint) * EXP2_SCALE)
        weights = jnp.exp2((scores - joint) * EXP2_SCALE)
        weight_sum = jnp.sum(weights, axis=0, keepdims=True)
        fresh = lax.dot_general(
            values, weights.astype(BF16), (((0,), (0,)), ((), ())), preferred_element_type=F32
        )
        if first:
            total[h, :, lanes] = weight_sum
            acc[h, :, lanes] = fresh
        else:
            total[h, :, lanes] = total[h, :, lanes] * factor + weight_sum
            acc[h, :, lanes] = acc[h, :, lanes] * factor + fresh
        top[h, :, lanes] = joint

    def scored(keys, queries):
        return lax.dot_general(keys, queries, (((1,), (1,)), ((), ())), preferred_element_type=F32)

    def for_heads(body):
        for h in range(HEADS):
            body(h, pl.ds(h * HEAD, HEAD))

    everyone = pl.ds(0, TOK)

    def own_tokens(h, cols):
        update(h, everyone, scored(kv[0, :, cols], q[:, cols]), kv[1, :, cols], first=True)

    def level(number):
        def body(h, cols):
            update(h, everyone, scored(lvl[number, 0, :, cols], q[:, cols]), lvl[number, 1, :, cols])

        for_heads(body)

    def side(which, block):
        lanes = pl.ds(pl.multiple_of(block * LEAF, LEAF), LEAF)

        def body(h, cols):
            update(h, lanes, scored(halo[which, 0, :, cols], q[lanes, cols]), halo[which, 1, :, cols])

        for_heads(body)

    def deep(tiles):
        wide[...] = tiles[...].astype(F32).reshape(LEAF * UNIT, HEAD)

        def body(h, cols):
            keys = wide[pl.ds(h, LEAF, stride=UNIT), :].astype(BF16)
            values = wide[pl.ds(HEADS + h, LEAF, stride=UNIT), :].astype(BF16)
            update(h, everyone, scored(keys, q[:, cols]), values)

        for_heads(body)

    xl, xr, xo = lax.rem(x + 3, X), lax.rem(x + 1, X), lax.rem(x + 2, X)
    xp, xm = at(xr, y, z, c), at(xl, y, z, c)
    p5, p6, p7, p8 = (lambda i: t5.at[c, i]), (lambda i: t6.at[c, i]), (lambda i: t7.at[c, i]), (lambda i: t8.at[c, yp, i])
    h5 = lambda i, j: t5.at[c, i, j]
    h6 = lambda i, j: t6.at[c, i, pl.ds(2 * j, 2)]
    h7 = lambda i, j: t7.at[c, i, pl.ds(4 * j, 4)]

    def spread_x(part, first):
        send(part(x), part(x), first, xp)
        send(part(x), part(x), first + 1, xm)

    def relay_x(part, half, first):
        arrived(part(xl), first)
        send(half(xl, 0), half(xl, 0), first + 2, xp)
        arrived(part(xr), first + 1)
        send(half(xr, 1), half(xr, 1), first + 3, xm)

    def whole_x(half, first):
        arrived(half(xo, 0), first + 2)
        arrived(half(xo, 1), first + 3)

    def far_sends():
        await_count(far_sem, count([later for _, later in far_peers]))
        for copy in far:
            copy.start()
        arrived(ybuf.at[pl.ds(0, 2)], 0)
        arrived(ybuf.at[pl.ds(2, 1)], 1)
        for copy in gather:
            copy.start()


    send(unit.at[pl.ds(12, 2)], ybuf.at[pl.ds(0, 2)], 0, at(x, y1, z, c))
    send(unit.at[pl.ds(14, 1)], ybuf.at[pl.ds(2, 1)], 1, at(x, y2, z, c))
    send(own.at[:, pl.ds(128, 64)], lvl.at[1, :, mine], 6, at(x, y, z1, c))
    send(own.at[:, pl.ds(224, 16)], lvl.at[3, :, rows(c * 64, 16)], 2, at(x3, y, z, c))
    send(own.at[:, pl.ds(192, 32)], lvl.at[2, :, rows(c * 64, 32)], 3, at(x1, y, z, c))

    @pl.when(steps)
    def _():
        step_copy.start()


    @pl.when(end_zhi < zhi)
    def _():
        end_copy.start()

    send(own.at[:, pl.ds(0, 128)], lvl.at[0], 4, mate)
    send(kv.at[:, rows((1 - c) * LEAF, LEAF)], halo.at[c], 5, mate)

    @pl.when(zhi >= 2)
    def _():
        far_sends()

    loads[2].wait()
    for_heads(own_tokens)
    arrived(lvl.at[1, :, mine], 6)
    send(lvl.at[1, :, mine], lvl.at[1, :, mine], 15, mate)
    passed = jnp.concatenate([average[:32, :64], average[128:144, :64]])
    for i in range(2):
        derived[i] = jnp.dot(passed, lvl[1, i, mine], preferred_element_type=F32).astype(BF16)
    send(derived.at[:, pl.ds(32, 16)], lvl.at[3, :, rows(c * 64 + 16, 16)], 26, at(x3, y, z, c))
    send(derived.at[:, pl.ds(0, 32)], lvl.at[2, :, rows(c * 64 + 32, 32)], 12, at(x1, y, z, c))
    arrived(lvl.at[0], 4)
    level(0)
    arrived(halo.at[1 - c], 5)
    side(1 - c, 1 - c)

    @pl.when(zhi < 2)
    def _():
        far_sends()


    @pl.when(end_zhi > zhi)
    def _():
        end_copy.start()

    zbuf[z] = ybuf[...]
    arrived(lvl.at[3, :, rows(c * 64, 16)], 2)
    arrived(lvl.at[3, :, rows(c * 64 + 16, 16)], 26)
    send(lvl.at[3, :, rows(c * 64, 32)], lvl.at[3, :, rows(c * 64 + 32, 32)], 11, at(x1, y, z, c))
    arrived(zbuf.at[pl.ds(0, 7)], 10)
    t8[c, yp, x] = zbuf[:, 2]
    t7[c, x] = zbuf[:, 0:2]
    for d in (1, 2, 3):
        send(p8(x), p8(x), 34 + d, at(lax.rem(x + d, X), y, z, c))
    spread_x(p7, 39)
    arrived(t5.at[c, x], 8)
    spread_x(p5, 27)
    arrived(t6.at[c, x], 9)
    spread_x(p6, 31)

    @pl.when(passes)
    def _():
        arrived(transit, 43)
        pass_copy.start()


    @pl.when(jnp.logical_not(outer))
    def _():
        inner_copy.start()

    arrived(lvl.at[2, :, rows(c * 64, 32)], 3)
    arrived(lvl.at[2, :, rows(c * 64 + 32, 32)], 12)
    send(lvl.at[2, :, mine], lvl.at[2, :, mine], 14, mate)
    arrived(lvl.at[3, :, rows(c * 64 + 32, 32)], 11)
    send(lvl.at[3, :, mine], lvl.at[3, :, mine], 13, mate)
    arrived(lvl.at[2, :, other], 14)
    level(2)
    arrived(lvl.at[1, :, other], 15)
    level(1)
    for d in (1, 2, 3):
        arrived(p8(lax.rem(x + X - d, X)), 34 + d)
    send(t8.at[c, yp], t8.at[c, yp], 20, at(x, y1, z, c))
    send(t8.at[c, yp], t8.at[c, yp], 21, mate)
    relay_x(p7, h7, 39)
    relay_x(p5, h5, 27)
    relay_x(p6, h6, 31)
    arrived(lvl.at[3, :, other], 13)
    level(3)
    arrived(t8.at[c, 1 - yp], 20)
    send(t8.at[c, 1 - yp], t8.at[c, 1 - yp], 25, mate)
    whole_x(h7, 39)
    send(t7.at[c], t7.at[c], 22, mate)
    whole_x(h5, 27)
    send(t5.at[c], t5.at[c], 24, mate)
    whole_x(h6, 31)
    send(t6.at[c], t6.at[c], 23, mate)
    arrived(t8.at[1 - c, yp], 21)
    arrived(t8.at[1 - c, 1 - yp], 25)
    deep(t8)
    arrived(t7.at[1 - c], 22)
    deep(t7)
    arrived(t5.at[1 - c], 24)
    deep(t5)
    arrived(t6.at[1 - c], 23)
    deep(t6)
    arrived(halo.at[c], 7)

    @pl.when((place + c > 0) & (place + c < 256))
    def _():
        side(c, c)


    def finish(h, cols):
        out_ref[:, cols] = (acc[h] / total[h]).T.astype(BF16)

    for_heads(finish)

    @pl.when(passes)
    def _():
        pass_copy.wait_send()

    for copy in [inner_copy] + far + gather + started:
        copy.wait_send()


def on_device(queries, keys, values):
    return pl.pallas_call(
        kernel,
        out_shape=jax.ShapeDtypeStruct((TOK, FEAT), BF16),
        in_specs=[pl.BlockSpec(memory_space=pl.ANY)] * 3,
        out_specs=pl.BlockSpec(memory_space=pltpu.VMEM),
        scratch_shapes=[
            pltpu.VMEM((TOK, FEAT), BF16),
            pltpu.VMEM((2, TOK, FEAT), BF16),
            pltpu.VMEM((2, 2, LEAF, FEAT), BF16),
            pltpu.VMEM((2, LEAF, FEAT), BF16),
            pltpu.VMEM((2, TOK, FEAT), BF16),
            pltpu.VMEM((4, 2, LEAF, FEAT), BF16),
            pltpu.VMEM((2, 48, FEAT), BF16),
            pltpu.VMEM((16, UNIT, HEAD), BF16),
            pltpu.VMEM((3, UNIT, HEAD), BF16),
            pltpu.VMEM((Z, 3, UNIT, HEAD), BF16),
            pltpu.VMEM((CORES, X, 2, 8, UNIT, HEAD), BF16),
            pltpu.VMEM((CORES, X, 4, 4, UNIT, HEAD), BF16),
            pltpu.VMEM((CORES, X, Z, 2, UNIT, HEAD), BF16),
            pltpu.VMEM((CORES, 2, X, Z, UNIT, HEAD), BF16),
            pltpu.VMEM((TOK, HEAD), F32),
            pltpu.VMEM((LEAF * UNIT, HEAD), F32),
            pltpu.VMEM((HEADS, HEAD, TOK), F32),
            pltpu.VMEM((HEADS, 1, TOK), F32),
            pltpu.VMEM((HEADS, 1, TOK), F32),
            pltpu.SemaphoreType.DMA((3,)),
            pltpu.SemaphoreType.DMA((101,)),
            pltpu.SemaphoreType.DMA((44,)),
            pltpu.SemaphoreType.REGULAR,
            pltpu.SemaphoreType.REGULAR,
        ],
        compiler_params=pltpu.CompilerParams(
            collective_id=0, has_side_effects=True, vmem_limit_bytes=24 * 1024 * 1024
        ),
    )(*[pltpu.with_memory_space_constraint(a, pltpu.HBM) for a in (queries, keys, values)])


def solution(mesh):
    spec = P(("seq", "sub"), None)
    return jax.shard_map(on_device, mesh=mesh, in_specs=(spec, spec, spec), out_specs=spec, check_vma=False)
```

```python
import math

import jax
import jax.numpy as jnp
from jax import lax
from jax.experimental import pallas as pl
from jax.experimental.pallas import tpu as pltpu
from jax.sharding import PartitionSpec as P

HEADS = 8
HEAD = 128
LEAF = 128
TOK = 256
FEAT = HEADS * HEAD
UNIT = 2 * HEADS
X, Y, Z, CORES = 4, 4, 8, 2
MESH = pl.DeviceIdType.MESH
F32 = jnp.float32
BF16 = jnp.bfloat16
EXP2_SCALE = math.log2(math.e) / math.sqrt(HEAD)
HIDDEN = -1e30


def averaging_matrix():
    row = lax.broadcasted_iota(jnp.int32, (TOK, TOK), 0)
    tok = lax.broadcasted_iota(jnp.int32, (TOK, TOK), 1)
    result = jnp.zeros((TOK, TOK), F32)
    base = 0
    for level in range(1, 9):
        count = TOK >> level
        first = (row - base) * (1 << level)
        hit = (row >= base) & (row < base + count) & (tok >= first) & (tok < first + (1 << level))
        result = jnp.where(hit, 2.0**-level, result)
        base += count
    return result.astype(BF16)


def kernel(
    q_hbm,
    k_hbm,
    v_hbm,
    out_ref,
    q,
    kv,
    halo,
    transit,
    own,
    lvl,
    derived,
    unit,
    ybuf,
    zbuf,
    t5,
    t6,
    t7,
    t8,
    spread,
    wide,
    acc,
    top,
    total,
    in_sem,
    send_sem,
    recv_sem,
    near_sem,
    far_sem,
):
    seq, sub = lax.axis_index("seq"), lax.axis_index("sub")
    x = lax.rem(seq, X)
    zhi = lax.rem(seq // X, Z // 2)
    y = seq // (X * Z // 2)
    c = lax.rem(sub, CORES)
    zlo = sub // CORES
    z = zhi * 2 + zlo
    place = seq * 4 + sub

    def at(xx, yy, zz, cc):
        return {"seq": (yy * (Z // 2) + zz // 2) * X + xx, "sub": lax.rem(zz, 2) * CORES + cc}

    loads = [
        pltpu.make_async_copy(k_hbm, kv.at[0], in_sem.at[0]),
        pltpu.make_async_copy(v_hbm, kv.at[1], in_sem.at[1]),
        pltpu.make_async_copy(q_hbm, q, in_sem.at[2]),
    ]
    for load in loads:
        load.start()

    x1 = x + 1 - 2 * lax.rem(x, 2)
    x3 = X - 1 - x
    y1 = y + 1 - 2 * lax.rem(y, 2)
    y2 = lax.rem(y + 2, Y)
    yp = lax.rem(y, 2)
    z1 = z + 1 - 2 * zlo
    mate = at(x, y, z, 1 - c)
    zhi1 = zhi + 1 - 2 * lax.rem(zhi, 2)
    end_place = lax.rem(place + 1 + 254 * (1 - c), 256)
    end = {"seq": end_place // 4, "sub": lax.rem(end_place, 4)}
    end_zhi = lax.rem(end_place // 16, Z // 2)
    end_near = end_zhi == zhi

    cross = at(x, y, z1, 1 - c)
    near = [(mate, c == 0), (at(x, y, z1, c), zlo == 0), (cross, zlo == 0), (at(x, y1, z, c), y1 > y), (at(x, y2, z, c), y2 > y)]
    near += [(at(xx, y, z, c), xx > x) for xx in [lax.rem(x + d, X) for d in (1, 2, 3)]]
    far_peers = [
        (at(x, y, zz * 2 + j, c), zz > zhi, 4 - d)
        for d, zz in [(d, lax.rem(zhi + d, Z // 2)) for d in (3, 2, 1)]
        for j in range(2)
    ]
    others = [peer for peer, _, _ in far_peers]
    end_far = jnp.logical_not(end_near)
    far_peers += [(end, end_zhi > zhi, 0)]

    barrier = pltpu.get_barrier_semaphore()

    def tell(sem, peer, when):
        @pl.when(when)
        def _():
            pl.semaphore_signal(sem, inc=1, device_id=peer, device_id_type=MESH)

    def count(flags):
        return sum(flag.astype(jnp.int32) for flag in flags)

    def await_count(sem, amount):
        @pl.when(amount > 0)
        def _():
            pl.semaphore_wait(sem, amount)

    for peer, later, *_ in far_peers + near:
        tell(barrier, peer, later)
    await_count(
        barrier,
        count([jnp.logical_not(later) for _, later, *_ in near + far_peers[:-1]]) + (end_zhi < zhi).astype(jnp.int32),
    )
    for peer, later, group in far_peers[:-1]:
        tell(far_sem.at[group], peer, jnp.logical_not(later))
    tell(far_sem.at[0], end, end_zhi < zhi)
    for peer, later in near:
        tell(near_sem, peer, jnp.logical_not(later))

    loads[0].wait()
    loads[1].wait()
    average = averaging_matrix()
    for i in range(2):
        for j in range(4):
            cols = pl.ds(j * 256, 256)
            coarse = jnp.dot(average, kv[i, :, cols], preferred_element_type=F32)
            own[i, :, cols] = coarse.astype(BF16)
            for hh in range(2):
                spread[pl.ds((i * HEADS + j * 2 + hh) * 16, 16), :] = coarse[240:, hh * HEAD : (hh + 1) * HEAD]
    for r in range(16):
        unit[r] = spread[pl.ds(r, UNIT, stride=16), :].astype(BF16)

    await_count(near_sem, count([later for _, later in near]))

    started = []

    def copy_to(src, dst, recv, peer, slot):
        return pltpu.make_async_remote_copy(
            src_ref=src,
            dst_ref=dst,
            send_sem=send_sem.at[slot],
            recv_sem=recv_sem.at[recv],
            device_id=peer,
            device_id_type=MESH,
        )

    def send(src, dst, recv, peer):
        copy = copy_to(src, dst, recv, peer, 14 + len(started))
        copy.start()
        started.append(copy)

    def arrived(ref, recv):
        pltpu.make_async_copy(ref, ref, recv_sem.at[recv]).wait()

    def rows(start, count):
        return pl.ds(pl.multiple_of(start, 16), count)

    mine, other = rows(c * 64, 64), rows((1 - c) * 64, 64)
    outer = c == zlo
    edge = kv.at[:, rows(c * LEAF, LEAF)]
    end_copy = copy_to(edge, halo.at[1 - c], 7, end, 0)
    inner_copy = copy_to(edge, halo.at[1 - c], 7, cross, 0)
    step_copy = copy_to(edge, transit, 43, at(lax.rem(x + 3 + 2 * c, X), y, z, c), 0)
    pass_copy = copy_to(transit, halo.at[1 - c], 7, cross, 100)
    steps = outer & end_near
    passes = outer & (x != 3 * (1 - c))
    far = [copy_to(unit.at[pl.ds(8, 4)], t6.at[c, x, lax.rem(z, 4)], 9, at(x, y, (1 - zhi // 2) * 4 + j, c), 1 + j) for j in range(4)]
    far += [copy_to(unit.at[pl.ds(0, 8)], t5.at[c, x, zlo], 8, at(x, y, zhi1 * 2 + j, c), 5 + j) for j in range(2)]
    gather = [copy_to(ybuf, zbuf.at[z], 10, peer, 7 + j) for j, peer in enumerate(others + [at(x, y, z1, c)])]

    def update(h, lanes, scores, values, first=False):
        high = jnp.max(scores, axis=0, keepdims=True)
        if first:
            joint = high
        else:
            old = top[h, :, lanes]
            joint = jnp.maximum(old, high)
            factor = jnp.exp2((old - joint) * EXP2_SCALE)
        weights = jnp.exp2((scores - joint) * EXP2_SCALE)
        weight_sum = jnp.sum(weights, axis=0, keepdims=True)
        fresh = lax.dot_general(
            values, weights.astype(BF16), (((0,), (0,)), ((), ())), preferred_element_type=F32
        )
        if first:
            total[h, :, lanes] = weight_sum
            acc[h, :, lanes] = fresh
        else:
            total[h, :, lanes] = total[h, :, lanes] * factor + weight_sum
            acc[h, :, lanes] = acc[h, :, lanes] * factor + fresh
        top[h, :, lanes] = joint

    def scored(keys, queries):
        return lax.dot_general(keys, queries, (((1,), (1,)), ((), ())), preferred_element_type=F32)

    def for_heads(body):
        for h in range(HEADS):
            body(h, pl.ds(h * HEAD, HEAD))

    everyone = pl.ds(0, TOK)

    def own_tokens(h, cols):
        update(h, everyone, scored(kv[0, :, cols], q[:, cols]), kv[1, :, cols], first=True)

    def level(number):
        def body(h, cols):
            update(h, everyone, scored(lvl[number, 0, :, cols], q[:, cols]), lvl[number, 1, :, cols])

        for_heads(body)

    def side(which, block):
        lanes = pl.ds(pl.multiple_of(block * LEAF, LEAF), LEAF)

        def body(h, cols):
            update(h, lanes, scored(halo[which, 0, :, cols], q[lanes, cols]), halo[which, 1, :, cols])

        for_heads(body)

    def deep(tiles):
        wide[...] = tiles[...].astype(F32).reshape(LEAF * UNIT, HEAD)

        def body(h, cols):
            keys = wide[pl.ds(h, LEAF, stride=UNIT), :].astype(BF16)
            values = wide[pl.ds(HEADS + h, LEAF, stride=UNIT), :].astype(BF16)
            update(h, everyone, scored(keys, q[:, cols]), values)

        for_heads(body)

    xl, xr, xo = lax.rem(x + 3, X), lax.rem(x + 1, X), lax.rem(x + 2, X)
    xp, xm = at(xr, y, z, c), at(xl, y, z, c)
    p5, p6, p7, p8 = (lambda i: t5.at[c, i]), (lambda i: t6.at[c, i]), (lambda i: t7.at[c, i]), (lambda i: t8.at[c, yp, i])
    h5 = lambda i, j: t5.at[c, i, j]
    h6 = lambda i, j: t6.at[c, i, pl.ds(2 * j, 2)]
    h7 = lambda i, j: t7.at[c, i, pl.ds(4 * j, 4)]

    def spread_x(part, first):
        send(part(x), part(x), first, xp)
        send(part(x), part(x), first + 1, xm)

    def relay_x(part, half, first):
        arrived(part(xl), first)
        send(half(xl, 0), half(xl, 0), first + 2, xp)
        arrived(part(xr), first + 1)
        send(half(xr, 1), half(xr, 1), first + 3, xm)

    def whole_x(half, first):
        arrived(half(xo, 0), first + 2)
        arrived(half(xo, 1), first + 3)

    def far_sends():
        await_count(far_sem.at[0], (end_zhi > zhi).astype(jnp.int32))
        await_count(far_sem.at[1], 2 * (zhi == 1).astype(jnp.int32))
        await_count(far_sem.at[2], 2 * (zhi < 2).astype(jnp.int32))
        await_count(far_sem.at[3], 2 * (zhi == 0).astype(jnp.int32))
        for copy in far[:4]:
            copy.start()
        arrived(ybuf.at[pl.ds(0, 2)], 0)
        arrived(ybuf.at[pl.ds(2, 1)], 1)
        for copy in gather:
            copy.start()


    send(unit.at[pl.ds(12, 2)], ybuf.at[pl.ds(0, 2)], 0, at(x, y1, z, c))
    send(unit.at[pl.ds(14, 1)], ybuf.at[pl.ds(2, 1)], 1, at(x, y2, z, c))
    send(own.at[:, pl.ds(128, 64)], lvl.at[1, :, mine], 6, at(x, y, z1, c))
    send(own.at[:, pl.ds(224, 16)], lvl.at[3, :, rows(c * 64, 16)], 2, at(x3, y, z, c))
    send(own.at[:, pl.ds(192, 32)], lvl.at[2, :, rows(c * 64, 32)], 3, at(x1, y, z, c))

    @pl.when(steps)
    def _():
        step_copy.start()


    @pl.when(end_zhi < zhi)
    def _():
        end_copy.start()

    send(own.at[:, pl.ds(0, 128)], lvl.at[0], 4, mate)
    send(kv.at[:, rows((1 - c) * LEAF, LEAF)], halo.at[c], 5, mate)
    loads[2].wait()
    for_heads(own_tokens)

    await_count(far_sem.at[1], 2 * (lax.rem(zhi, 2) == 0).astype(jnp.int32))
    for copy in far[4:]:
        copy.start()

    @pl.when(zhi >= 2)
    def _():
        far_sends()

    arrived(lvl.at[0], 4)
    level(0)
    arrived(halo.at[1 - c], 5)
    side(1 - c, 1 - c)
    arrived(lvl.at[1, :, mine], 6)
    send(lvl.at[1, :, mine], lvl.at[1, :, mine], 15, mate)
    passed = jnp.concatenate([average[:32, :64], average[128:144, :64]])
    for i in range(2):
        derived[i] = jnp.dot(passed, lvl[1, i, mine], preferred_element_type=F32).astype(BF16)
    send(derived.at[:, pl.ds(32, 16)], lvl.at[3, :, rows(c * 64 + 16, 16)], 26, at(x3, y, z, c))
    send(derived.at[:, pl.ds(0, 32)], lvl.at[2, :, rows(c * 64 + 32, 32)], 12, at(x1, y, z, c))
    arrived(t5.at[c, x], 8)
    spread_x(p5, 27)

    @pl.when(zhi < 2)
    def _():
        far_sends()


    @pl.when(end_zhi > zhi)
    def _():
        end_copy.start()

    zbuf[z] = ybuf[...]
    arrived(lvl.at[3, :, rows(c * 64, 16)], 2)
    arrived(lvl.at[3, :, rows(c * 64 + 16, 16)], 26)
    send(lvl.at[3, :, rows(c * 64, 32)], lvl.at[3, :, rows(c * 64 + 32, 32)], 11, at(x1, y, z, c))
    relay_x(p5, h5, 27)
    arrived(zbuf.at[pl.ds(0, 7)], 10)
    t8[c, yp, x] = zbuf[:, 2]
    t7[c, x] = zbuf[:, 0:2]
    for d in (1, 2, 3):
        send(p8(x), p8(x), 34 + d, at(lax.rem(x + d, X), y, z, c))
    spread_x(p7, 39)

    @pl.when(passes)
    def _():
        arrived(transit, 43)
        pass_copy.start()

    arrived(t6.at[c, x], 9)
    spread_x(p6, 31)

    @pl.when(jnp.logical_not(outer))
    def _():
        inner_copy.start()

    arrived(lvl.at[2, :, rows(c * 64, 32)], 3)
    arrived(lvl.at[2, :, rows(c * 64 + 32, 32)], 12)
    send(lvl.at[2, :, mine], lvl.at[2, :, mine], 14, mate)
    arrived(lvl.at[2, :, other], 14)
    level(2)
    whole_x(h5, 27)
    send(t5.at[c], t5.at[c], 24, mate)
    arrived(lvl.at[3, :, rows(c * 64 + 32, 32)], 11)
    send(lvl.at[3, :, mine], lvl.at[3, :, mine], 13, mate)
    arrived(lvl.at[1, :, other], 15)
    level(1)
    for d in (1, 2, 3):
        arrived(p8(lax.rem(x + X - d, X)), 34 + d)
    send(t8.at[c, yp], t8.at[c, yp], 20, at(x, y1, z, c))
    send(t8.at[c, yp], t8.at[c, yp], 21, mate)
    relay_x(p7, h7, 39)
    relay_x(p6, h6, 31)
    arrived(lvl.at[3, :, other], 13)
    level(3)
    arrived(t8.at[c, 1 - yp], 20)
    send(t8.at[c, 1 - yp], t8.at[c, 1 - yp], 25, mate)
    whole_x(h7, 39)
    send(t7.at[c], t7.at[c], 22, mate)
    whole_x(h6, 31)
    send(t6.at[c], t6.at[c], 23, mate)
    arrived(t5.at[1 - c], 24)
    deep(t5)
    arrived(t8.at[1 - c, yp], 21)
    arrived(t8.at[1 - c, 1 - yp], 25)
    deep(t8)
    arrived(t7.at[1 - c], 22)
    deep(t7)
    arrived(t6.at[1 - c], 23)
    deep(t6)
    arrived(halo.at[c], 7)

    @pl.when((place + c > 0) & (place + c < 256))
    def _():
        side(c, c)


    def finish(h, cols):
        out_ref[:, cols] = (acc[h] / total[h]).T.astype(BF16)

    for_heads(finish)

    @pl.when(passes)
    def _():
        pass_copy.wait_send()

    for copy in [inner_copy] + far + gather + started:
        copy.wait_send()


def on_device(queries, keys, values):
    return pl.pallas_call(
        kernel,
        out_shape=jax.ShapeDtypeStruct((TOK, FEAT), BF16),
        in_specs=[pl.BlockSpec(memory_space=pl.ANY)] * 3,
        out_specs=pl.BlockSpec(memory_space=pltpu.VMEM),
        scratch_shapes=[
            pltpu.VMEM((TOK, FEAT), BF16),
            pltpu.VMEM((2, TOK, FEAT), BF16),
            pltpu.VMEM((2, 2, LEAF, FEAT), BF16),
            pltpu.VMEM((2, LEAF, FEAT), BF16),
            pltpu.VMEM((2, TOK, FEAT), BF16),
            pltpu.VMEM((4, 2, LEAF, FEAT), BF16),
            pltpu.VMEM((2, 48, FEAT), BF16),
            pltpu.VMEM((16, UNIT, HEAD), BF16),
            pltpu.VMEM((3, UNIT, HEAD), BF16),
            pltpu.VMEM((Z, 3, UNIT, HEAD), BF16),
            pltpu.VMEM((CORES, X, 2, 8, UNIT, HEAD), BF16),
            pltpu.VMEM((CORES, X, 4, 4, UNIT, HEAD), BF16),
            pltpu.VMEM((CORES, X, Z, 2, UNIT, HEAD), BF16),
            pltpu.VMEM((CORES, 2, X, Z, UNIT, HEAD), BF16),
            pltpu.VMEM((TOK, HEAD), F32),
            pltpu.VMEM((LEAF * UNIT, HEAD), F32),
            pltpu.VMEM((HEADS, HEAD, TOK), F32),
            pltpu.VMEM((HEADS, 1, TOK), F32),
            pltpu.VMEM((HEADS, 1, TOK), F32),
            pltpu.SemaphoreType.DMA((3,)),
            pltpu.SemaphoreType.DMA((101,)),
            pltpu.SemaphoreType.DMA((44,)),
            pltpu.SemaphoreType.REGULAR,
            pltpu.SemaphoreType.REGULAR((4,)),
        ],
        compiler_params=pltpu.CompilerParams(
            collective_id=0, has_side_effects=True, vmem_limit_bytes=24 * 1024 * 1024
        ),
    )(*[pltpu.with_memory_space_constraint(a, pltpu.HBM) for a in (queries, keys, values)])


def solution(mesh):
    spec = P(("seq", "sub"), None)
    return jax.shard_map(on_device, mesh=mesh, in_specs=(spec, spec, spec), out_specs=spec, check_vma=False)
```

```python
import math

import jax
import jax.numpy as jnp
from jax import lax
from jax.experimental import pallas as pl
from jax.experimental.pallas import tpu as pltpu
from jax.sharding import PartitionSpec as P

HEADS = 8
HEAD = 128
LEAF = 128
TOK = 256
FEAT = HEADS * HEAD
UNIT = 2 * HEADS
X, Y, Z, CORES = 4, 4, 8, 2
MESH = pl.DeviceIdType.MESH
F32 = jnp.float32
BF16 = jnp.bfloat16
EXP2_SCALE = math.log2(math.e) / math.sqrt(HEAD)
HIDDEN = -1e30


def averaging_matrix():
    row = lax.broadcasted_iota(jnp.int32, (TOK, TOK), 0)
    tok = lax.broadcasted_iota(jnp.int32, (TOK, TOK), 1)
    result = jnp.zeros((TOK, TOK), F32)
    base = 0
    for level in range(1, 9):
        count = TOK >> level
        first = (row - base) * (1 << level)
        hit = (row >= base) & (row < base + count) & (tok >= first) & (tok < first + (1 << level))
        result = jnp.where(hit, 2.0**-level, result)
        base += count
    return result.astype(BF16)


def kernel(
    q_hbm,
    k_hbm,
    v_hbm,
    out_ref,
    q,
    kv,
    halo,
    transit,
    own,
    lvl,
    derived,
    unit,
    ybuf,
    zbuf,
    t5,
    t6,
    t7,
    t8,
    spread,
    wide,
    acc,
    top,
    total,
    in_sem,
    send_sem,
    recv_sem,
    near_sem,
    far_sem,
):
    seq, sub = lax.axis_index("seq"), lax.axis_index("sub")
    x = lax.rem(seq, X)
    zhi = lax.rem(seq // X, Z // 2)
    y = seq // (X * Z // 2)
    c = lax.rem(sub, CORES)
    zlo = sub // CORES
    z = zhi * 2 + zlo
    place = seq * 4 + sub

    def at(xx, yy, zz, cc):
        return {"seq": (yy * (Z // 2) + zz // 2) * X + xx, "sub": lax.rem(zz, 2) * CORES + cc}

    loads = [
        pltpu.make_async_copy(k_hbm, kv.at[0], in_sem.at[0]),
        pltpu.make_async_copy(v_hbm, kv.at[1], in_sem.at[1]),
        pltpu.make_async_copy(q_hbm, q, in_sem.at[2]),
    ]
    for load in loads:
        load.start()

    x1 = x + 1 - 2 * lax.rem(x, 2)
    x3 = X - 1 - x
    y1 = y + 1 - 2 * lax.rem(y, 2)
    y2 = lax.rem(y + 2, Y)
    yp = lax.rem(y, 2)
    z1 = z + 1 - 2 * zlo
    mate = at(x, y, z, 1 - c)
    zhi1 = zhi + 1 - 2 * lax.rem(zhi, 2)
    end_place = lax.rem(place + 1 + 254 * (1 - c), 256)
    end = {"seq": end_place // 4, "sub": lax.rem(end_place, 4)}
    end_zhi = lax.rem(end_place // 16, Z // 2)
    end_near = end_zhi == zhi

    cross = at(x, y, z1, 1 - c)
    near = [(mate, c == 0), (at(x, y, z1, c), zlo == 0), (cross, zlo == 0), (at(x, y1, z, c), y1 > y), (at(x, y2, z, c), y2 > y)]
    near += [(at(xx, y, z, c), xx > x) for xx in [lax.rem(x + d, X) for d in (1, 2, 3)]]
    far_peers = [
        (at(x, y, zz * 2 + j, c), zz > zhi, 4 - d)
        for d, zz in [(d, lax.rem(zhi + d, Z // 2)) for d in (3, 2, 1)]
        for j in range(2)
    ]
    others = [peer for peer, _, _ in far_peers]
    end_far = jnp.logical_not(end_near)
    far_peers += [(end, end_zhi > zhi, 0)]

    barrier = pltpu.get_barrier_semaphore()

    def tell(sem, peer, when):
        @pl.when(when)
        def _():
            pl.semaphore_signal(sem, inc=1, device_id=peer, device_id_type=MESH)

    def count(flags):
        return sum(flag.astype(jnp.int32) for flag in flags)

    def await_count(sem, amount):
        @pl.when(amount > 0)
        def _():
            pl.semaphore_wait(sem, amount)

    for peer, later, *_ in far_peers + near:
        tell(barrier, peer, later)
    await_count(
        barrier,
        count([jnp.logical_not(later) for _, later, *_ in near + far_peers[:-1]]) + (end_zhi < zhi).astype(jnp.int32),
    )
    for peer, later, group in far_peers[:-1]:
        tell(far_sem.at[group], peer, jnp.logical_not(later))
    tell(far_sem.at[0], end, end_zhi < zhi)
    for peer, later in near:
        tell(near_sem, peer, jnp.logical_not(later))

    loads[0].wait()
    loads[1].wait()
    average = averaging_matrix()
    for i in range(2):
        for j in range(4):
            cols = pl.ds(j * 256, 256)
            coarse = jnp.dot(average, kv[i, :, cols], preferred_element_type=F32)
            own[i, :, cols] = coarse.astype(BF16)
            for hh in range(2):
                spread[pl.ds((i * HEADS + j * 2 + hh) * 16, 16), :] = coarse[240:, hh * HEAD : (hh + 1) * HEAD]
    for r in range(16):
        unit[r] = spread[pl.ds(r, UNIT, stride=16), :].astype(BF16)

    await_count(near_sem, count([later for _, later in near]))

    started = []

    def copy_to(src, dst, recv, peer, slot):
        return pltpu.make_async_remote_copy(
            src_ref=src,
            dst_ref=dst,
            send_sem=send_sem.at[slot],
            recv_sem=recv_sem.at[recv],
            device_id=peer,
            device_id_type=MESH,
        )

    def send(src, dst, recv, peer):
        copy = copy_to(src, dst, recv, peer, 14 + len(started))
        copy.start()
        started.append(copy)

    def arrived(ref, recv):
        pltpu.make_async_copy(ref, ref, recv_sem.at[recv]).wait()

    def rows(start, count):
        return pl.ds(pl.multiple_of(start, 16), count)

    mine, other = rows(c * 64, 64), rows((1 - c) * 64, 64)
    outer = c == zlo
    edge = kv.at[:, rows(c * LEAF, LEAF)]
    end_copy = copy_to(edge, halo.at[1 - c], 7, end, 0)
    inner_copy = copy_to(edge, halo.at[1 - c], 7, cross, 0)
    step_copy = copy_to(edge, transit, 43, at(lax.rem(x + 3 + 2 * c, X), y, z, c), 0)
    pass_copy = copy_to(transit, halo.at[1 - c], 7, cross, 100)
    steps = outer & end_near
    passes = outer & (x != 3 * (1 - c))
    far = [copy_to(unit.at[pl.ds(8, 4)], t6.at[c, x, lax.rem(z, 4)], 9, at(x, y, (1 - zhi // 2) * 4 + j, c), 1 + j) for j in range(4)]
    far += [copy_to(unit.at[pl.ds(0, 8)], t5.at[c, x, zlo], 8, at(x, y, zhi1 * 2 + j, c), 5 + j) for j in range(2)]
    gather = [copy_to(ybuf, zbuf.at[z], 10, peer, 7 + j) for j, peer in enumerate(others + [at(x, y, z1, c)])]

    def update(h, lanes, scores, values, first=False):
        high = jnp.max(scores, axis=0, keepdims=True)
        if first:
            joint = high
        else:
            old = top[h, :, lanes]
            joint = jnp.maximum(old, high)
            factor = jnp.exp2((old - joint) * EXP2_SCALE)
        weights = jnp.exp2((scores - joint) * EXP2_SCALE)
        weight_sum = jnp.sum(weights, axis=0, keepdims=True)
        fresh = lax.dot_general(
            values, weights.astype(BF16), (((0,), (0,)), ((), ())), preferred_element_type=F32
        )
        if first:
            total[h, :, lanes] = weight_sum
            acc[h, :, lanes] = fresh
        else:
            total[h, :, lanes] = total[h, :, lanes] * factor + weight_sum
            acc[h, :, lanes] = acc[h, :, lanes] * factor + fresh
        top[h, :, lanes] = joint

    def scored(keys, queries):
        return lax.dot_general(keys, queries, (((1,), (1,)), ((), ())), preferred_element_type=F32)

    def for_heads(body):
        for h in range(HEADS):
            body(h, pl.ds(h * HEAD, HEAD))

    everyone = pl.ds(0, TOK)

    def own_tokens(h, cols):
        update(h, everyone, scored(kv[0, :, cols], q[:, cols]), kv[1, :, cols], first=True)

    def level(number):
        def body(h, cols):
            update(h, everyone, scored(lvl[number, 0, :, cols], q[:, cols]), lvl[number, 1, :, cols])

        for_heads(body)

    def side(which, block):
        lanes = pl.ds(pl.multiple_of(block * LEAF, LEAF), LEAF)

        def body(h, cols):
            update(h, lanes, scored(halo[which, 0, :, cols], q[lanes, cols]), halo[which, 1, :, cols])

        for_heads(body)

    def deep(tiles):
        wide[...] = tiles[...].astype(F32).reshape(LEAF * UNIT, HEAD)

        def body(h, cols):
            keys = wide[pl.ds(h, LEAF, stride=UNIT), :].astype(BF16)
            values = wide[pl.ds(HEADS + h, LEAF, stride=UNIT), :].astype(BF16)
            update(h, everyone, scored(keys, q[:, cols]), values)

        for_heads(body)

    xl, xr, xo = lax.rem(x + 3, X), lax.rem(x + 1, X), lax.rem(x + 2, X)
    xp, xm = at(xr, y, z, c), at(xl, y, z, c)
    p5, p6, p7, p8 = (lambda i: t5.at[c, i]), (lambda i: t6.at[c, i]), (lambda i: t7.at[c, i]), (lambda i: t8.at[c, yp, i])
    h5 = lambda i, j: t5.at[c, i, j]
    h6 = lambda i, j: t6.at[c, i, pl.ds(2 * j, 2)]
    h7 = lambda i, j: t7.at[c, i, pl.ds(4 * j, 4)]

    def spread_x(part, first):
        send(part(x), part(x), first, xp)
        send(part(x), part(x), first + 1, xm)

    def relay_x(part, half, first):
        arrived(part(xl), first)
        send(half(xl, 0), half(xl, 0), first + 2, xp)
        arrived(part(xr), first + 1)
        send(half(xr, 1), half(xr, 1), first + 3, xm)

    def whole_x(half, first):
        arrived(half(xo, 0), first + 2)
        arrived(half(xo, 1), first + 3)

    def far_sends():
        await_count(far_sem.at[0], (end_zhi > zhi).astype(jnp.int32))
        await_count(far_sem.at[1], 2 * (zhi == 1).astype(jnp.int32))
        await_count(far_sem.at[2], 2 * (zhi < 2).astype(jnp.int32))
        await_count(far_sem.at[3], 2 * (zhi == 0).astype(jnp.int32))
        for copy in far[:4]:
            copy.start()
        arrived(ybuf.at[pl.ds(0, 2)], 0)
        arrived(ybuf.at[pl.ds(2, 1)], 1)
        for copy in gather:
            copy.start()


    send(unit.at[pl.ds(12, 2)], ybuf.at[pl.ds(0, 2)], 0, at(x, y1, z, c))
    send(unit.at[pl.ds(14, 1)], ybuf.at[pl.ds(2, 1)], 1, at(x, y2, z, c))
    send(own.at[:, pl.ds(128, 64)], lvl.at[1, :, mine], 6, at(x, y, z1, c))
    send(own.at[:, pl.ds(224, 16)], lvl.at[3, :, rows(c * 64, 16)], 2, at(x3, y, z, c))
    send(own.at[:, pl.ds(192, 32)], lvl.at[2, :, rows(c * 64, 32)], 3, at(x1, y, z, c))

    @pl.when(steps)
    def _():
        step_copy.start()


    @pl.when(end_zhi < zhi)
    def _():
        end_copy.start()

    send(own.at[:, pl.ds(0, 128)], lvl.at[0], 4, mate)
    send(kv.at[:, rows((1 - c) * LEAF, LEAF)], halo.at[c], 5, mate)
    loads[2].wait()
    for_heads(own_tokens)

    await_count(far_sem.at[1], 2 * (lax.rem(zhi, 2) == 0).astype(jnp.int32))
    for copy in far[4:]:
        copy.start()

    @pl.when(zhi >= 2)
    def _():
        far_sends()

    arrived(lvl.at[0], 4)
    level(0)
    arrived(halo.at[1 - c], 5)
    side(1 - c, 1 - c)
    arrived(lvl.at[1, :, mine], 6)
    send(lvl.at[1, :, mine], lvl.at[1, :, mine], 15, mate)
    passed = jnp.concatenate([average[:32, :64], average[128:144, :64]])
    for i in range(2):
        derived[i] = jnp.dot(passed, lvl[1, i, mine], preferred_element_type=F32).astype(BF16)
    send(derived.at[:, pl.ds(32, 16)], lvl.at[3, :, rows(c * 64 + 16, 16)], 26, at(x3, y, z, c))
    send(derived.at[:, pl.ds(0, 32)], lvl.at[2, :, rows(c * 64 + 32, 32)], 12, at(x1, y, z, c))
    arrived(t5.at[c, x], 8)
    spread_x(p5, 27)

    @pl.when(zhi < 2)
    def _():
        far_sends()


    @pl.when(end_zhi > zhi)
    def _():
        end_copy.start()

    zbuf[z] = ybuf[...]
    arrived(lvl.at[3, :, rows(c * 64, 16)], 2)
    arrived(lvl.at[3, :, rows(c * 64 + 16, 16)], 26)
    send(lvl.at[3, :, rows(c * 64, 32)], lvl.at[3, :, rows(c * 64 + 32, 32)], 11, at(x1, y, z, c))
    relay_x(p5, h5, 27)
    arrived(zbuf.at[pl.ds(0, 7)], 10)
    t8[c, yp, x] = zbuf[:, 2]
    t7[c, x] = zbuf[:, 0:2]
    for d in (1, 2, 3):
        send(p8(x), p8(x), 34 + d, at(lax.rem(x + d, X), y, z, c))
    spread_x(p7, 39)

    @pl.when(passes)
    def _():
        arrived(transit, 43)
        pass_copy.start()

    arrived(t6.at[c, x], 9)
    spread_x(p6, 31)

    @pl.when(jnp.logical_not(outer))
    def _():
        inner_copy.start()

    arrived(lvl.at[2, :, rows(c * 64, 32)], 3)
    arrived(lvl.at[2, :, rows(c * 64 + 32, 32)], 12)
    send(lvl.at[2, :, mine], lvl.at[2, :, mine], 14, mate)
    arrived(lvl.at[2, :, other], 14)
    level(2)
    whole_x(h5, 27)
    send(t5.at[c], t5.at[c], 24, mate)
    arrived(lvl.at[3, :, rows(c * 64 + 32, 32)], 11)
    send(lvl.at[3, :, mine], lvl.at[3, :, mine], 13, mate)
    arrived(lvl.at[1, :, other], 15)
    level(1)
    for d in (1, 2, 3):
        arrived(p8(lax.rem(x + X - d, X)), 34 + d)
    send(t8.at[c, yp], t8.at[c, yp], 20, at(x, y1, z, c))
    send(t8.at[c, yp], t8.at[c, yp], 21, mate)
    relay_x(p7, h7, 39)
    relay_x(p6, h6, 31)
    arrived(lvl.at[3, :, other], 13)
    level(3)
    arrived(t8.at[c, 1 - yp], 20)
    send(t8.at[c, 1 - yp], t8.at[c, 1 - yp], 25, mate)
    whole_x(h7, 39)
    send(t7.at[c], t7.at[c], 22, mate)
    whole_x(h6, 31)
    send(t6.at[c], t6.at[c], 23, mate)
    arrived(t5.at[1 - c], 24)
    deep(t5)
    arrived(t8.at[1 - c, yp], 21)
    arrived(t8.at[1 - c, 1 - yp], 25)
    deep(t8)
    arrived(t7.at[1 - c], 22)
    deep(t7)
    arrived(t6.at[1 - c], 23)
    deep(t6)
    arrived(halo.at[c], 7)

    @pl.when((place + c > 0) & (place + c < 256))
    def _():
        side(c, c)


    def finish(h, cols):
        out_ref[:, cols] = (acc[h] * (1.0 / total[h])).T.astype(BF16)

    for_heads(finish)

    @pl.when(passes)
    def _():
        pass_copy.wait_send()

    for copy in [inner_copy] + far + gather + started:
        copy.wait_send()


def on_device(queries, keys, values):
    return pl.pallas_call(
        kernel,
        out_shape=jax.ShapeDtypeStruct((TOK, FEAT), BF16),
        in_specs=[pl.BlockSpec(memory_space=pl.ANY)] * 3,
        out_specs=pl.BlockSpec(memory_space=pltpu.VMEM),
        scratch_shapes=[
            pltpu.VMEM((TOK, FEAT), BF16),
            pltpu.VMEM((2, TOK, FEAT), BF16),
            pltpu.VMEM((2, 2, LEAF, FEAT), BF16),
            pltpu.VMEM((2, LEAF, FEAT), BF16),
            pltpu.VMEM((2, TOK, FEAT), BF16),
            pltpu.VMEM((4, 2, LEAF, FEAT), BF16),
            pltpu.VMEM((2, 48, FEAT), BF16),
            pltpu.VMEM((16, UNIT, HEAD), BF16),
            pltpu.VMEM((3, UNIT, HEAD), BF16),
            pltpu.VMEM((Z, 3, UNIT, HEAD), BF16),
            pltpu.VMEM((CORES, X, 2, 8, UNIT, HEAD), BF16),
            pltpu.VMEM((CORES, X, 4, 4, UNIT, HEAD), BF16),
            pltpu.VMEM((CORES, X, Z, 2, UNIT, HEAD), BF16),
            pltpu.VMEM((CORES, 2, X, Z, UNIT, HEAD), BF16),
            pltpu.VMEM((TOK, HEAD), F32),
            pltpu.VMEM((LEAF * UNIT, HEAD), F32),
            pltpu.VMEM((HEADS, HEAD, TOK), F32),
            pltpu.VMEM((HEADS, 1, TOK), F32),
            pltpu.VMEM((HEADS, 1, TOK), F32),
            pltpu.SemaphoreType.DMA((3,)),
            pltpu.SemaphoreType.DMA((101,)),
            pltpu.SemaphoreType.DMA((44,)),
            pltpu.SemaphoreType.REGULAR,
            pltpu.SemaphoreType.REGULAR((4,)),
        ],
        compiler_params=pltpu.CompilerParams(
            collective_id=0, has_side_effects=True, vmem_limit_bytes=24 * 1024 * 1024
        ),
    )(*[pltpu.with_memory_space_constraint(a, pltpu.HBM) for a in (queries, keys, values)])


def solution(mesh):
    spec = P(("seq", "sub"), None)
    return jax.shard_map(on_device, mesh=mesh, in_specs=(spec, spec, spec), out_specs=spec, check_vma=False)
```
